256 devices in a mesh: patch: 16 (over x, y_lo, core), var: 16 (over z, y_hi).
Axes of the slice: x: 4, y: 4 (y_hi: 2, y_lo: 2; y = y_hi * 2 + y_lo), z: 8, core: 2. Of those that a mesh axis runs over, the one named last changes fastest.
Arguments:
- fields: bfloat16 [32, 48, 4, 1024], P(None, 'var', None, 'patch'), may hold values from -8 to 8
- var_ids: int32 [48], replicated, may hold values from 0 to 47, each once
- lead_index: int32 [32], P('var'), may hold values from 0 to 15
- embed_weight: bfloat16 [48, 4, 1024], replicated, may hold values from -3 to 3
- var_embed: bfloat16 [48, 1024], replicated, may hold values from -3 to 3
- agg_query: bfloat16 [1024], replicated, may hold values from -28 to 28
- agg_key: bfloat16 [1024, 1024], replicated, may hold values from -0.1875 to 0.1875
- agg_value: bfloat16 [1024, 1024], replicated, may hold values from -0.1875 to 0.1875
- agg_out: bfloat16 [1024, 1024], replicated, may hold values from -0.1875 to 0.1875
- pos_embed: bfloat16 [1024, 1024], P('patch'), may hold values from -3 to 6
- lead_table: bfloat16 [16, 1024], replicated, may hold values from -3 to 3
- norm_gain: bfloat16 [1024], replicated, may hold values from 0.099609375 to 1.8984375
- qkv_weight: bfloat16 [3, 1024, 1024], P(None, None, 'patch'), may hold values from -0.5 to 0.5
- out_weight: bfloat16 [1024, 1024], replicated, may hold values from -0.1875 to 0.1875
- cotangent: bfloat16 [32, 1024, 1024], P('var', 'patch'), may hold values from -0.3125 to 0.3125
Outputs:
- layer_out: bfloat16 [32, 1024, 1024], P('var', 'patch')
- grad_qkv: float32 [3, 1024, 1024], P(None, 'var', 'patch')
The draws below stay inside these ranges and needn't reach their ends.
Inputs may be any that keep to these rules, and one draw needn't show every extreme that they name: `var_ids`: each variable id stands in exactly one slot.
All inputs are finite; a program needn't handle non-finite values.
Results may differ from the reference program's by a relative error of at most 0.015.
The reference program's roundings to bfloat16 on the way count: a program that leaves them out, or rounds other values in their place, can miss the bound.
Values may be sent and summed in bfloat16 or wider, within the bound.
No kernel may reach another device: no remote copies, remote signals or barrier semaphores. Data moves between devices by JAX's collectives and lax.ppermute only.
A program may use at most 128 MiB of HBM per device.

```python
import jax
import jax.numpy as jnp
from jax import lax

D = 1024
H = 16
HD = 64
V = 48
PIX = 4
NLEAD = 16
B = 32
P_SIZE = 1024


def draw_fields(key, part):
    key = jax.random.fold_in(key, 11)
    key_base = jax.random.fold_in(key, 0)
    full_shape = (B, V, PIX, P_SIZE)
    values = jnp.clip(jax.random.normal(key_base, full_shape, jnp.float32), -6.0, 6.0)
    return values.astype(jnp.bfloat16)


def draw_agg_query(key, part):
    key = jax.random.fold_in(key, 12)
    values = jnp.clip(jax.random.normal(key, (D,), jnp.float32), -6.0, 6.0)
    return values.astype(jnp.bfloat16)


def draw_pos_embed(key, part):
    key = jax.random.fold_in(key, 13)
    key_base = jax.random.fold_in(key, 0)
    values = jnp.clip(0.5 * jax.random.normal(key_base, (P_SIZE, D), jnp.float32), -3.0, 3.0)
    return values.astype(jnp.bfloat16)


def draw_qkv_weight(key, part):
    key = jax.random.fold_in(key, 14)
    key_base = jax.random.fold_in(key, 0)
    factor = D ** (-0.5)
    values = jax.random.normal(key_base, (3, D, D), jnp.float32) * factor
    values = jnp.clip(values, -0.5, 0.5)
    return values.astype(jnp.bfloat16)


def touch_ends(values, own_key, low, high):
    longest = values.shape.index(max(values.shape))
    spots = []
    for shift in (0, 1):
        where = [jax.random.randint(jax.random.fold_in(own_key, axis), (), 0, length) for axis, length in enumerate(values.shape)]
        where[longest] = (where[longest] + shift) % values.shape[longest]
        spots.append(tuple(where))
    return values.at[spots[0]].set(low).at[spots[1]].set(high)


def levels(rng, shape, shards, low, top_value):
    factor_of, own = 1.0, jax.random.fold_in(rng, 6)
    for position, blocks in shards:
        heights = jnp.exp(jax.random.uniform(jax.random.fold_in(own, position), (blocks,), jnp.float32, low / len(shards), top_value / len(shards)))
        factor_of = factor_of * jnp.repeat(heights, shape[position] // blocks).reshape([-1 if axis == position else 1 for axis in range(len(shape))])
    return factor_of


def scatter_about(own_key, shape, scale, most, pieces=(), kind=jnp.bfloat16):
    loudness = levels(own_key, shape, pieces, -0.22, 0.18) if pieces else 1.0
    result = jax.random.normal(own_key, shape, jnp.float32) * scale * loudness
    return jnp.minimum(jnp.maximum(result, -most), most).astype(kind)


def setup_inputs(seed: int = 0) -> dict:
    arg_keys = jax.random.split(jax.random.key(seed), 16)
    return {
        "fields": draw_fields(jax.random.fold_in(arg_keys[15], 71), 0),
        "var_ids": jax.random.permutation(arg_keys[1], V).astype(jnp.int32),
        "lead_index": touch_ends(jax.random.randint(arg_keys[2], (B,), 0, NLEAD), jax.random.fold_in(arg_keys[2], 1), 0, NLEAD - 1).astype(jnp.int32),
        "embed_weight": scatter_about(arg_keys[3], (V, PIX, D), PIX ** -0.5, 3.0),
        "var_embed": scatter_about(arg_keys[4], (V, D), 0.5, 3.0),
        "agg_query": draw_agg_query(jax.random.fold_in(arg_keys[15], 71), 0),
        "agg_key": scatter_about(arg_keys[6], (D, D), D ** -0.5, 0.1875),
        "agg_value": scatter_about(arg_keys[7], (D, D), D ** -0.5, 0.1875),
        "agg_out": scatter_about(arg_keys[8], (D, D), D ** -0.5, 0.1875),
        "pos_embed": draw_pos_embed(jax.random.fold_in(arg_keys[15], 71), 0),
        "lead_table": scatter_about(arg_keys[10], (NLEAD, D), 0.5, 3.0),
        "norm_gain": jnp.clip(1.0 + 0.18 * jax.random.normal(arg_keys[11], (D,), jnp.float32), 0.099609375, 1.8984375).astype(jnp.bfloat16),
        "qkv_weight": draw_qkv_weight(jax.random.fold_in(arg_keys[15], 71), 0),
        "out_weight": scatter_about(arg_keys[13], (D, D), D ** -0.5, 0.1875),
        "cotangent": scatter_about(arg_keys[14], (B, P_SIZE, D), (4.0 / (B * P_SIZE) ** 0.5), 0.3125, ((0, 16), (1, 16))),
    }


def layer_norm(tokens, norm_gain):
    center = tokens - lax.optimization_barrier(jnp.mean(tokens, axis=-1, keepdims=True))
    spread = lax.optimization_barrier(jnp.mean(center * center, axis=-1, keepdims=True))
    return (center * lax.rsqrt(spread + 1e-05) * norm_gain.astype(jnp.float32)).astype(jnp.bfloat16)

def reference(fields, var_ids, lead_index, embed_weight, var_embed, agg_query, agg_key, agg_value, agg_out, pos_embed, lead_table, norm_gain, qkv_weight, out_weight, cotangent):
    highest = lax.Precision.HIGHEST
    scaling = HD ** (-0.5)
    table = jnp.concatenate([embed_weight[var_ids].astype(jnp.float32), var_embed[var_ids].astype(jnp.float32)[:, None, :]], axis=1)
    query_heads = agg_query.astype(jnp.float32).reshape(H, HD) * scaling
    key_query = jnp.einsum('dhe,he->dh', agg_key.astype(jnp.float32).reshape(D, H, HD), query_heads, precision=highest)
    score_table = jnp.einsum('vkd,dh->vkh', table, key_query, precision=highest)
    value_table = jnp.einsum('vkd,de->vke', table, agg_value.astype(jnp.float32), precision=highest).reshape(V, PIX + 1, H, HD)

    def one_sample(grad_total, inputs):
        pixels, lead, cot_rows = inputs
        padded = jnp.concatenate([pixels.astype(jnp.float32), jnp.ones((V, 1, P_SIZE), jnp.float32)], axis=1)
        agg_scores = jnp.einsum('vkp,vkh->vhp', padded, score_table, precision=highest)
        agg_probs = jax.nn.softmax(agg_scores, axis=0)
        mixing = agg_probs[:, None, :, :] * padded[:, :, None, :]
        pooled = jnp.einsum('vkhp,vkhe->phe', mixing, value_table, precision=highest).reshape(P_SIZE, D).astype(jnp.bfloat16)
        tokens = jnp.dot(pooled, agg_out, preferred_element_type=jnp.float32) + pos_embed.astype(jnp.float32) + lead_table[lead].astype(jnp.float32)[None, :]
        normed = layer_norm(tokens, norm_gain)
        projected = [jnp.dot(normed, qkv_weight[idx], preferred_element_type=jnp.float32).astype(jnp.bfloat16).reshape(P_SIZE, H, HD) for idx in range(3)]
        queries, key_rows, value_rows = projected
        scores = jnp.einsum('qhe,khe->hqk', queries.astype(jnp.float32), key_rows.astype(jnp.float32)) * scaling
        att_probs = jax.nn.softmax(scores, axis=-1)
        probs_low = att_probs.astype(jnp.bfloat16)
        context = jnp.einsum('hqk,khe->qhe', probs_low.astype(jnp.float32), value_rows.astype(jnp.float32)).astype(jnp.bfloat16).reshape(P_SIZE, D)
        layer_rows = (tokens + jnp.dot(context, out_weight, preferred_element_type=jnp.float32)).astype(jnp.bfloat16)
        grad_context = jnp.dot(cot_rows, out_weight.T, preferred_element_type=jnp.float32).astype(jnp.bfloat16).reshape(P_SIZE, H, HD).astype(jnp.float32)
        grad_probs = jnp.einsum('qhe,khe->hqk', grad_context, value_rows.astype(jnp.float32))
        grad_values = jnp.einsum('hqk,qhe->khe', probs_low.astype(jnp.float32), grad_context).astype(jnp.bfloat16)
        grad_scores = (att_probs * (grad_probs - lax.optimization_barrier(jnp.sum(att_probs * grad_probs, axis=-1, keepdims=True))) * scaling).astype(jnp.bfloat16).astype(jnp.float32)
        grad_queries = jnp.einsum('hqk,khe->qhe', grad_scores, key_rows.astype(jnp.float32)).astype(jnp.bfloat16)
        grad_keys = jnp.einsum('hqk,qhe->khe', grad_scores, queries.astype(jnp.float32)).astype(jnp.bfloat16)
        stacked = jnp.stack([grad_queries, grad_keys, grad_values]).reshape(3, P_SIZE, D)
        grad_total = grad_total + jnp.stack([jnp.dot(normed.T, stacked[idx], preferred_element_type=jnp.float32) for idx in range(3)])
        return (grad_total, layer_rows)
    grad_qkv, layer_out = lax.scan(one_sample, jnp.zeros((3, D, D), jnp.float32), (fields, lead_index, cotangent))
    return (layer_out, grad_qkv)
```

```python
import functools

import jax
import jax.numpy as jnp
from jax import lax
from jax.experimental import pallas as pl
from jax.experimental.pallas import tpu as pltpu
from jax.sharding import PartitionSpec as P

H = 16
HD = 64
V = 48
PIX = 4
D = 1024
ROWS = 64
BLOCK = 256
F32 = jnp.float32
BF16 = jnp.bfloat16
VMEM_LIMIT = 56 * 1024 * 1024

NN = (((1,), (0,)), ((), ()))
NT = (((1,), (1,)), ((), ()))
TN = (((0,), (0,)), ((), ()))


def mm(a, b, dims=NN):
    return lax.dot_general(a, b, dims, preferred_element_type=F32)


def split2(x):
    high = x.astype(BF16)
    return high, (x - high.astype(F32)).astype(BF16)


def prep_kernel(
    target_ref, query_ref, embed_ref, var_embed_ref, key_ref, value_ref, out_w_ref, cot_ref,
    place_ref, score_ref, table_ref, grad_ref,
):
    count = place_ref.shape[1]
    rows = lax.broadcasted_iota(jnp.int32, (V * PIX, count), 0)
    place_ref[...] = (target_ref[...] == rows).astype(F32).astype(BF16)
    row = lax.broadcasted_iota(jnp.int32, (V * PIX, V * PIX), 0)
    col = lax.broadcasted_iota(jnp.int32, (V * PIX, V * PIX), 1)
    order = ((row % V) * PIX + row // V == col).astype(F32).astype(BF16)
    table = jnp.concatenate(
        [mm(order, embed_ref[...]).astype(BF16), var_embed_ref[...]], axis=0
    )
    values = mm(table, value_ref[...]).T
    high, low = split2(values)
    for h in range(H):
        table_ref[h, :HD, :] = high[h * HD:(h + 1) * HD]
        table_ref[h, HD:, :] = low[h * HD:(h + 1) * HD]
    head = lax.broadcasted_iota(jnp.int32, (H, D), 0)
    feature = lax.broadcasted_iota(jnp.int32, (H, D), 1)
    query = jnp.where(feature // HD == head, query_ref[...].astype(F32) * HD ** (-0.5), 0.0)
    key_query = mm(query.astype(BF16), key_ref[...], NT)
    first = key_query.astype(BF16)
    rest = key_query - first.astype(F32)
    second = rest.astype(BF16)
    third = (rest - second.astype(F32)).astype(BF16)
    score_ref[...] = mm(table, first, NT) + (mm(table, second, NT) + mm(table, third, NT))
    grad = mm(cot_ref[...], out_w_ref[...], NT).astype(BF16)
    for j in range(H):
        r = (j % 2) * ROWS
        own = grad[r:r + ROWS, j * HD:(j + 1) * HD]
        other = grad[r:r + ROWS, (j ^ 1) * HD:((j ^ 1) + 1) * HD]
        grad_ref[j] = jnp.concatenate([own, other], axis=1)


def token_kernel(
    place_ref, fields_ref, score_ref, table_ref, agg_out_ref, pos_ref, lead_ref, lead_table_ref, gain_ref,
    core_ref, tokens_ref, keep_ref, send_ref, normed_ref,
):
    pixels = mm(place_ref[...], fields_ref[...])
    parts = [pixels[k * V:(k + 1) * V] for k in range(PIX)]
    pooled = []
    for h in range(H):
        column = lambda k: score_ref[k * V:(k + 1) * V, h:h + 1]
        scores = column(PIX) + parts[0] * column(0)
        for k in range(1, PIX):
            scores = scores + parts[k] * column(k)
        probs = jnp.exp(scores - jnp.max(scores, axis=0, keepdims=True))
        probs = probs / jnp.sum(probs, axis=0, keepdims=True)
        mixing = jnp.concatenate([probs * part for part in parts] + [probs], axis=0)
        high, low = split2(mixing)
        both = mm(table_ref[h], high)
        pooled.append((both[:HD] + (both[HD:] + mm(table_ref[h, :HD], low))).astype(BF16))
    pooled = jnp.concatenate(pooled, axis=0)
    tokens = mm(pooled, agg_out_ref[...], TN)
    row = lax.broadcasted_iota(jnp.int32, (2 * ROWS, 16), 0)
    col = lax.broadcasted_iota(jnp.int32, (2 * ROWS, 16), 1)
    lead = jnp.where(row < ROWS, lead_ref[0], lead_ref[1])
    lead_rows = mm((lead == col).astype(F32).astype(BF16), lead_table_ref[...])
    pos = pos_ref[...].astype(F32)
    tokens = tokens + jnp.concatenate([pos, pos], axis=0) + lead_rows
    tokens_ref[...] = tokens
    center = tokens - jnp.mean(tokens, axis=-1, keepdims=True)
    spread = jnp.mean(center * center, axis=-1, keepdims=True)
    normed_ref[...] = (center * lax.rsqrt(spread + 1e-05) * gain_ref[...].astype(F32)).astype(BF16)
    own = pl.multiple_of(core_ref[0] * ROWS, ROWS)
    other = pl.multiple_of((1 - core_ref[0]) * ROWS, ROWS)
    keep_ref[...] = normed_ref[pl.ds(own, ROWS), :]
    send_ref[...] = normed_ref[pl.ds(other, ROWS), :]


def attention_kernel(pieces, *refs):
    n = len(pieces)
    piece_refs = refs[:n]
    (offset_ref, weight_ref, grad_ctx_ref, context_ref, own_ref, other_ref,
     x_ref, q_ref, k_ref, v_ref, dq_ref, dk_ref, dv_ref, w_ref, sem) = refs[n:]
    copies = []
    for i, (ref, start) in enumerate(zip(piece_refs, pieces)):
        copies.append(pltpu.make_async_copy(ref, x_ref.at[pl.ds(start, ref.shape[0])], sem.at[i]))
        copies[-1].start()
    for copy in copies:
        copy.wait()
    offsets = [pl.multiple_of(offset_ref[i], ROWS) for i in range(H)]
    projected = mm(x_ref[...], weight_ref[...]).astype(BF16)
    for i in range(H):
        rows = pl.ds(offsets[i], ROWS)
        here = projected[i * ROWS:(i + 1) * ROWS]
        q_ref[rows, :] = here[:, :128] * jnp.asarray(HD ** (-0.5), BF16)
        k_ref[rows, :] = here[:, 128:256]
        v_ref[rows, :] = here[:, 256:]
    keys = k_ref[...]
    values = v_ref[...]
    keys_t = keys.T
    values_t = values.T
    dk_ref[...] = jnp.zeros_like(dk_ref)
    dv_ref[...] = jnp.zeros_like(dv_ref)
    lane = lax.broadcasted_iota(jnp.int32, (BLOCK, 128), 1)

    def step(i, carry):
        rows = pl.ds(pl.multiple_of(i * BLOCK, BLOCK), BLOCK)
        queries = q_ref[rows, :]
        grads = grad_ctx_ref[rows, :]
        context, dq, low, ds, gs, qs = [], [], [], [], [], []
        for h in range(2):
            mine = lane // HD == h
            q = jnp.where(mine, queries, jnp.zeros_like(queries))
            g = jnp.where(mine, grads, jnp.zeros_like(grads))
            scores = mm(keys, q, NT)
            e = jnp.exp(scores - jnp.max(scores, axis=0, keepdims=True))
            probs = e * (1.0 / jnp.sum(e, axis=0, keepdims=True))
            probs_low = probs.astype(BF16)
            context.append(mm(values_t[h * HD:(h + 1) * HD], probs_low))
            dp = mm(values, g, NT)
            dots = jnp.sum(probs * dp, axis=0, keepdims=True)
            d = (probs * (dp - dots)).astype(BF16)
            dq.append(mm(keys_t[h * HD:(h + 1) * HD], d))
            low.append(probs_low)
            ds.append(d)
            gs.append(g)
            qs.append(q)
        context_ref[rows, :] = jnp.concatenate(context, axis=0).T.astype(BF16)
        dq_ref[rows, :] = (jnp.concatenate(dq, axis=0).T * HD ** (-0.5)).astype(BF16)
        dv_ref[...] += mm(jnp.concatenate(low, axis=1), jnp.concatenate(gs, axis=0))
        dk_ref[...] += mm(jnp.concatenate(ds, axis=1), jnp.concatenate(qs, axis=0))
        return carry

    lax.fori_loop(0, D // BLOCK, step, 0)
    for i in range(H):
        rows = pl.ds(offsets[i], ROWS)
        here = slice(i * ROWS, (i + 1) * ROWS)
        dq = dq_ref[rows, :]
        dk = dk_ref[rows, :].astype(BF16)
        dv = dv_ref[rows, :].astype(BF16)
        w_ref[here, 0:128] = jnp.concatenate([dq[:, :HD], dk[:, :HD]], axis=1)
        w_ref[here, 128:256] = jnp.concatenate([dq[:, HD:], dk[:, HD:]], axis=1)
        w_ref[here, 256:384] = dv
    grad = mm(x_ref[...], w_ref[...], TN)
    for j in range(H):
        top = grad[j * ROWS:j * ROWS + ROWS // 2, 256:]
        bottom = grad[j * ROWS + ROWS // 2:(j + 1) * ROWS, 256:]
        own_ref[j, :ROWS] = grad[j * ROWS:(j + 1) * ROWS, :128]
        own_ref[j, ROWS:] = jnp.concatenate([top[:, :HD], bottom[:, :HD]], axis=1)
        other_ref[j, :ROWS] = grad[j * ROWS:(j + 1) * ROWS, 128:256]
        other_ref[j, ROWS:] = jnp.concatenate([top[:, HD:], bottom[:, HD:]], axis=1)


def output_kernel(context_ref, out_w_ref, tokens_ref, out_ref):
    rows = []
    for s in range(2):
        parts = []
        for m in range(H // 2):
            part = context_ref[2 * m + s]
            if s:
                part = jnp.concatenate([part[:, HD:], part[:, :HD]], axis=1)
            parts.append(part)
        rows.append(jnp.concatenate(parts, axis=1))
    context = jnp.concatenate(rows, axis=0)
    out_ref[...] = (tokens_ref[...] + mm(context, out_w_ref[...])).astype(BF16)


def sum_kernel(parts_ref, out_ref):
    total = parts_ref[0].astype(F32)
    for j in range(1, H):
        total = total + parts_ref[j].astype(F32)
    out_ref[0] = total[:ROWS, :HD]
    out_ref[1] = total[:ROWS, HD:]
    out_ref[2, :ROWS // 2] = total[ROWS:, :HD]
    out_ref[2, ROWS // 2:] = total[ROWS:, HD:]


VM = pl.BlockSpec(memory_space=pltpu.VMEM)
SM = pl.BlockSpec(memory_space=pltpu.SMEM)
ANY = pl.BlockSpec(memory_space=pl.ANY)


def call(kernel, out, in_specs, name, scratch=()):
    return pl.pallas_call(
        kernel,
        out_shape=out,
        in_specs=in_specs,
        out_specs=jax.tree.map(lambda _: VM, out),
        scratch_shapes=list(scratch),
        compiler_params=pltpu.CompilerParams(vmem_limit_bytes=VMEM_LIMIT),
        name=name,
    )


def shape(dims, dtype):
    return jax.ShapeDtypeStruct(dims, dtype)


def on_device(
    fields, var_ids, lead_index, embed_weight, var_embed, agg_query, agg_key, agg_value, agg_out,
    pos_embed, lead_table, norm_gain, qkv_weight, out_weight, cotangent,
):
    place = lax.axis_index("patch")
    core = place % 2
    chip = place // 2
    pair = [(i, i ^ 1) for i in range(16)]
    across = [(i, i ^ 2) for i in range(16)]
    up = [(i, (i + 4) % 16) for i in range(16)]
    down = [(i, (i - 4) % 16) for i in range(16)]
    move = lambda a, perm: lax.ppermute(a, "patch", perm)

    sent = fields.reshape(16, 2, 3, PIX, ROWS).transpose(0, 2, 3, 1, 4).reshape(16, 12, 128)
    sent = jnp.pad(sent, ((0, 0), (0, 4), (0, 0)))
    owned = lax.all_to_all(sent, "var", split_axis=0, concat_axis=0, tiled=True).reshape(256, 128)
    target = var_ids.reshape(16, 3, 1) + V * jnp.arange(PIX, dtype=jnp.int32)[None, None, :]
    target = jnp.pad(target.reshape(16, 12), ((0, 0), (0, 4)), constant_values=-1).reshape(1, 256)

    other_weight = move(qkv_weight, pair)
    weight = jnp.concatenate([qkv_weight, other_weight], axis=2)
    weight = weight.transpose(1, 0, 2).reshape(D, 384)

    placing, score, table, grad_parts = call(
        prep_kernel,
        (shape((V * PIX, 256), BF16), shape((V * (PIX + 1), H), F32),
         shape((H, 2 * HD, V * (PIX + 1)), BF16), shape((H, ROWS, 128), BF16)),
        [VM] * 8, "prep",
    )(target, agg_query.reshape(1, D), embed_weight.reshape(V * PIX, D), var_embed, agg_key, agg_value,
      out_weight, cotangent.reshape(2 * ROWS, D))

    tokens, keep, send = call(
        token_kernel,
        (shape((2 * ROWS, D), F32), shape((ROWS, D), BF16), shape((ROWS, D), BF16)),
        [VM] * 6 + [SM] + [VM] * 2 + [SM], "tokens", [pltpu.VMEM((2 * ROWS, D), BF16)],
    )(placing, owned, score, table, agg_out, pos_embed, lead_index, lead_table, norm_gain.reshape(1, D),
      core.reshape(1))

    here = jnp.concatenate([keep, move(send, pair)], axis=0)
    y = move(here, across)
    left = move(here, up)
    right = move(here, down)
    grad_ctx = lax.all_to_all(grad_parts, "patch", split_axis=0, concat_axis=0, tiled=True)
    far0 = move(left[:64], up)
    far1 = move(right[64:], down)
    y_left = move(y, up)
    y_right = move(y, down)
    y_far0 = move(far0, across)
    y_far1 = move(y_left[64:96], up)
    y_far2 = move(y_right[96:], down)
    pieces = [here, y, left, right, y_left, y_right, far0, far1, y_far0, y_far1, y_far2]
    starts, at = [], 0
    for piece in pieces:
        starts.append(at)
        at += piece.shape[0]
    cx, cy = chip // 2, chip % 2
    chips = []
    for dx, dy in [(0, 0), (0, 1), (-1, 0), (1, 0), (-1, 1), (1, 1), (2, 0), (2, 1)]:
        chips.append(((cx + dx) % 4) * 2 + (cy + dy) % 2)
    chips = jnp.stack(chips)
    offsets = (chips[:, None] * 128 + jnp.stack([core, 1 - core])[None, :] * ROWS).reshape(16)

    scratch = [pltpu.VMEM((D, D), BF16)] + [pltpu.VMEM((D, 128), BF16)] * 4
    scratch += [pltpu.VMEM((D, 128), F32)] * 2 + [pltpu.VMEM((D, 384), BF16)]
    scratch += [pltpu.SemaphoreType.DMA((len(pieces),))]
    context, own, other = call(
        functools.partial(attention_kernel, tuple(starts)),
        (shape((D, 128), BF16), shape((H, 96, 128), F32), shape((H, 96, 128), F32)),
        [ANY] * len(pieces) + [SM, VM, VM], "attention", scratch,
    )(*pieces, offsets.astype(jnp.int32), weight, grad_ctx.reshape(D, 128))

    partial_grad = (own + move(other, pair)).astype(BF16)
    parts = lax.all_to_all(partial_grad, "var", split_axis=0, concat_axis=0, tiled=True)
    merged = lax.all_to_all(context.reshape(H, ROWS, 128), "patch", split_axis=0, concat_axis=0, tiled=True)
    layer_out = call(output_kernel, shape((2 * ROWS, D), BF16), [VM] * 3, "out")(merged, out_weight, tokens)
    grad_qkv = call(sum_kernel, shape((3, ROWS, HD), F32), [VM], "sum")(parts)
    return layer_out.reshape(2, ROWS, D), grad_qkv


def solution(mesh):
    in_specs = (
        P(None, "var", None, "patch"), P(), P("var"), P(), P(), P(), P(), P(), P(), P("patch", None), P(), P(),
        P(None, None, "patch"), P(), P("var", "patch", None),
    )
    out_specs = (P("var", "patch", None), P(None, "var", "patch"))
    return jax.shard_map(on_device, mesh=mesh, in_specs=in_specs, out_specs=out_specs, check_vma=False)
```

```python
import functools

import jax
import jax.numpy as jnp
from jax import lax
from jax.experimental import pallas as pl
from jax.experimental.pallas import tpu as pltpu
from jax.sharding import PartitionSpec as P

H = 16
HD = 64
V = 48
PIX = 4
D = 1024
ROWS = 64
F32 = jnp.float32
BF16 = jnp.bfloat16
PIECES = 10
MIB = 1024 * 1024
VMEM_MIB = 58

NN = (((1,), (0,)), ((), ()))
NT = (((1,), (1,)), ((), ()))
TN = (((0,), (0,)), ((), ()))


def mm(a, b, dims=NN):
    return lax.dot_general(a, b, dims, preferred_element_type=F32)


def split2(x):
    high = x.astype(BF16)
    return high, (x - high.astype(F32)).astype(BF16)


def fetch(pairs, sems, first=0):
    copies = [pltpu.make_async_copy(a, b, sems.at[first + i]) for i, (a, b) in enumerate(pairs)]
    for copy in copies:
        copy.start()
    return copies


def prep_kernel(
    ids_ref, query_ref, var_embed_ref, embed_hbm, value_hbm, key_hbm, cot_hbm, out_w_hbm,
    place_ref, score_ref, grad_ref, table_hbm,
    embed_ref, value_ref, key_ref, cot_ref, out_w_ref, table_ref, embed_rows_ref, sems,
):
    copies = fetch(
        [(embed_hbm, embed_ref), (value_hbm, value_ref), (key_hbm, key_ref), (cot_hbm, cot_ref), (out_w_hbm, out_w_ref)], sems
    )
    count = place_ref.shape[1]
    slot = lax.broadcasted_iota(jnp.int32, (V, count), 0)
    col = lax.broadcasted_iota(jnp.int32, (V, count), 1)
    here = ((col // 16) * 3 + (col % 16) // PIX == slot) & (col % 16 < 3 * PIX)
    ids = jnp.broadcast_to(ids_ref[...].reshape(1, V).astype(F32).astype(BF16), (8, V))
    variable = mm(ids, here.astype(F32).astype(BF16))[:1].astype(jnp.int32)
    row = lax.broadcasted_iota(jnp.int32, (V * PIX, count), 0)
    col = lax.broadcasted_iota(jnp.int32, (V * PIX, count), 1)
    match = (variable + V * (col % PIX) == row) & (col % 16 < 3 * PIX)
    place_ref[...] = match.astype(F32).astype(BF16)
    copies[0].wait()
    for n in range(V):
        embed_rows_ref[n * PIX:(n + 1) * PIX, :] = embed_ref[n].astype(F32)
    row = lax.broadcasted_iota(jnp.int32, (V * PIX, V * PIX), 0)
    col = lax.broadcasted_iota(jnp.int32, (V * PIX, V * PIX), 1)
    order = ((row % V) * PIX + row // V == col).astype(F32).astype(BF16)
    table = jnp.concatenate(
        [mm(order, embed_rows_ref[...].astype(BF16)).astype(BF16), var_embed_ref[...]], axis=0
    )
    copies[1].wait()
    values = mm(table, value_ref[...]).T
    high, low = split2(values)
    for h in range(H):
        table_ref[h, :HD, :] = high[h * HD:(h + 1) * HD]
        table_ref[h, HD:, :] = low[h * HD:(h + 1) * HD]
    saved = pltpu.make_async_copy(table_ref, table_hbm, sems.at[5])
    saved.start()
    head = lax.broadcasted_iota(jnp.int32, (H, D), 0)
    feature = lax.broadcasted_iota(jnp.int32, (H, D), 1)
    query = jnp.where(feature // HD == head, query_ref[...].astype(F32).reshape(1, D) * HD ** (-0.5), 0.0)
    copies[2].wait()
    key_query = mm(query.astype(BF16), key_ref[...], NT)
    first = key_query.astype(BF16)
    rest = key_query - first.astype(F32)
    second = rest.astype(BF16)
    third = (rest - second.astype(F32)).astype(BF16)
    score_ref[...] = mm(table, first, NT) + (mm(table, second, NT) + mm(table, third, NT))
    copies[3].wait()
    copies[4].wait()
    grad = mm(cot_ref[...].reshape(2 * ROWS, D), out_w_ref[...], NT).astype(BF16)
    for j in range(H):
        r = (j % 2) * ROWS
        own = grad[r:r + ROWS, j * HD:(j + 1) * HD]
        other = grad[r:r + ROWS, (j ^ 1) * HD:((j ^ 1) + 1) * HD]
        grad_ref[j] = jnp.concatenate([own, other], axis=1)
    saved.wait()


def token_kernel(
    place_ref, fields_ref, score_ref, table_hbm, agg_out_hbm, pos_ref, lead_ref, lead_table_ref, gain_ref,
    core_ref, tokens_ref, keep_ref, send_ref, normed_ref, rows_ref, table_ref, agg_out_ref, sems,
):
    copies = fetch([(table_hbm, table_ref), (agg_out_hbm, agg_out_ref)], sems)
    rows_ref[...] = jnp.zeros_like(rows_ref)
    for j in range(H):
        rows_ref[16 * j:16 * j + 3 * PIX, :] = fields_ref[j]
    pixels = mm(place_ref[...], rows_ref[...])
    parts = [pixels[k * V:(k + 1) * V] for k in range(PIX)]
    mixed = []
    for h in range(H):
        column = lambda k: score_ref[k * V:(k + 1) * V, h:h + 1]
        scores = column(PIX) + parts[0] * column(0)
        for k in range(1, PIX):
            scores = scores + parts[k] * column(k)
        probs = jnp.exp(scores - jnp.max(scores, axis=0, keepdims=True))
        probs = probs / jnp.sum(probs, axis=0, keepdims=True)
        mixing = jnp.concatenate([probs * part for part in parts] + [probs], axis=0)
        mixed.append(split2(mixing))
    copies[0].wait()
    pooled = []
    for h in range(H):
        high, low = mixed[h]
        both = mm(table_ref[h], high)
        pooled.append((both[:HD] + (both[HD:] + mm(table_ref[h, :HD], low))).astype(BF16))
    pooled = jnp.concatenate(pooled, axis=0)
    copies[1].wait()
    tokens = mm(pooled, agg_out_ref[...], TN)
    row = lax.broadcasted_iota(jnp.int32, (2 * ROWS, 16), 0)
    col = lax.broadcasted_iota(jnp.int32, (2 * ROWS, 16), 1)
    lead = jnp.where(row < ROWS, lead_ref[0], lead_ref[1])
    lead_rows = mm((lead == col).astype(F32).astype(BF16), lead_table_ref[...])
    pos = pos_ref[...].astype(F32)
    tokens = tokens + jnp.concatenate([pos, pos], axis=0) + lead_rows
    tokens_ref[...] = tokens
    center = tokens - jnp.mean(tokens, axis=-1, keepdims=True)
    spread = jnp.mean(center * center, axis=-1, keepdims=True)
    normed_ref[...] = (center * lax.rsqrt(spread + 1e-05) * gain_ref[...].astype(F32).reshape(1, D)).astype(BF16)
    own = pl.multiple_of(core_ref[0] * ROWS, ROWS)
    other = pl.multiple_of((1 - core_ref[0]) * ROWS, ROWS)
    keep_ref[...] = normed_ref[pl.ds(own, ROWS), :]
    send_ref[...] = normed_ref[pl.ds(other, ROWS), :]


def softmax_of(keys, queries):
    scores = mm(keys, queries, NT)
    e = jnp.exp(scores - jnp.max(scores, axis=0, keepdims=True))
    return e * (1.0 / jnp.sum(e, axis=0, keepdims=True))


def head_of(x, h):
    lane = lax.broadcasted_iota(jnp.int32, x.shape, 1)
    return jnp.where(lane // HD == h, x, jnp.zeros_like(x))


def gather_rows(pieces, x_ref):
    pairs, at = [], 0
    for piece in pieces:
        pairs.append((piece, x_ref.at[pl.ds(at, piece.shape[0])]))
        at += piece.shape[0]
    return pairs


def attention_kernel(*refs):
    pieces = refs[:PIECES]
    offset_ref, to_ref, own_w_ref, other_w_ref, grad_ctx_ref, own_ref, other_ref = refs[PIECES:PIECES + 7]
    part_refs = refs[PIECES + 7:PIECES + 11]
    x_ref, context_ref, q_ref, k_ref, v_ref, rows_ref, sems = refs[PIECES + 11:]
    copies = fetch(gather_rows(pieces, x_ref), sems)
    weight = jnp.concatenate([w for i in range(3) for w in (own_w_ref[i], other_w_ref[i])], axis=1)
    for copy in copies:
        copy.wait()
    projected = mm(x_ref[...], weight).astype(BF16)
    for i in range(H):
        rows = pl.ds(pl.multiple_of(offset_ref[i], ROWS), ROWS)
        here = projected[i * ROWS:(i + 1) * ROWS]
        q_ref[rows, :] = here[:, :128] * jnp.asarray(HD ** (-0.5), BF16)
        k_ref[rows, :] = here[:, 128:256]
        v_ref[rows, :] = here[:, 256:]
    keys, values = k_ref[...], v_ref[...]
    keys_t, values_t = keys.T, values.T
    context, dq, low, ds, gs, qs = [], [], [], [], [], []
    for h in range(2):
        queries = head_of(q_ref[...], h)
        grads = head_of(grad_ctx_ref[...], h)
        probs = softmax_of(keys, queries)
        probs_low = probs.astype(BF16)
        context.append(mm(values_t[h * HD:(h + 1) * HD], probs_low))
        dp = mm(values, grads, NT)
        dots = jnp.sum(probs * dp, axis=0, keepdims=True)
        d = (probs * (dp - dots)).astype(BF16)
        dq.append(mm(keys_t[h * HD:(h + 1) * HD], d))
        low.append(probs_low)
        ds.append(d)
        gs.append(grads)
        qs.append(queries)
    context_ref[...] = jnp.concatenate(context, axis=0).T.astype(BF16)
    for i in range(H):
        part_refs[i // 4][i % 4] = context_ref[pl.ds(pl.multiple_of(to_ref[i], ROWS), ROWS), :]
    dq = (jnp.concatenate(dq, axis=0).T * HD ** (-0.5)).astype(BF16)
    dv = mm(jnp.concatenate(low, axis=1), jnp.concatenate(gs, axis=0)).astype(BF16)
    dk = mm(jnp.concatenate(ds, axis=1), jnp.concatenate(qs, axis=0)).astype(BF16)
    rows_ref[:, :128] = jnp.concatenate([dq[:, :HD], dk[:, :HD]], axis=1)
    rows_ref[:, 128:256] = jnp.concatenate([dq[:, HD:], dk[:, HD:]], axis=1)
    rows_ref[:, 256:] = dv
    order = [rows_ref[pl.ds(pl.multiple_of(offset_ref[i], ROWS), ROWS), :] for i in range(H)]
    grad = mm(x_ref[...], jnp.concatenate(order, axis=0), TN).astype(BF16)
    for j in range(H):
        top = grad[j * ROWS:j * ROWS + ROWS // 2, 256:]
        bottom = grad[j * ROWS + ROWS // 2:(j + 1) * ROWS, 256:]
        own_ref[j, :ROWS] = grad[j * ROWS:(j + 1) * ROWS, :128]
        own_ref[j, ROWS:] = jnp.concatenate([top[:, :HD], bottom[:, :HD]], axis=1)
        other_ref[j, :ROWS] = grad[j * ROWS:(j + 1) * ROWS, 128:256]
        other_ref[j, ROWS:] = jnp.concatenate([top[:, HD:], bottom[:, HD:]], axis=1)


def output_kernel(from_ref, core_ref, *refs):
    near = refs[:4]
    along = refs[4:7]
    out_w_ref, tokens_ref, out_ref, context_ref = refs[7:]
    core = core_ref[0]
    for dx in range(4):
        for i in range(4):
            part = along[dx - 1][i] if dx else near[i][0]
            sample = core if i % 2 == 0 else 1 - core
            part = jnp.where(sample == 1, jnp.concatenate([part[:, HD:], part[:, :HD]], axis=1), part)
            context_ref[from_ref[dx * 2 + i // 2], pl.ds(pl.multiple_of(sample * ROWS, ROWS), ROWS), :] = part
    context = jnp.concatenate([context_ref[m] for m in range(H // 2)], axis=1)
    out_ref[...] = (tokens_ref[...] + mm(context, out_w_ref[...])).astype(BF16)


def sum_kernel(parts_ref, out_ref):
    total = parts_ref[0].astype(F32)
    for j in range(1, H):
        total = total + parts_ref[j].astype(F32)
    out_ref[0] = total[:ROWS, :HD]
    out_ref[1] = total[:ROWS, HD:]
    out_ref[2, :ROWS // 2] = total[ROWS:, :HD]
    out_ref[2, ROWS // 2:] = total[ROWS:, HD:]


VM = pl.BlockSpec(memory_space=pltpu.VMEM)
SM = pl.BlockSpec(memory_space=pltpu.SMEM)
ANY = pl.BlockSpec(memory_space=pl.ANY)


def call(kernel, out, in_specs, name, scratch=(), out_specs=None, mib=VMEM_MIB):
    return pl.pallas_call(
        kernel,
        out_shape=out,
        in_specs=in_specs,
        out_specs=out_specs or jax.tree.map(lambda _: VM, out),
        scratch_shapes=list(scratch),
        compiler_params=pltpu.CompilerParams(vmem_limit_bytes=mib * MIB),
        name=name,
    )


def shape(dims, dtype):
    return jax.ShapeDtypeStruct(dims, dtype)


def on_device(
    fields, var_ids, lead_index, embed_weight, var_embed, agg_query, agg_key, agg_value, agg_out,
    pos_embed, lead_table, norm_gain, qkv_weight, out_weight, cotangent,
):
    place = lax.axis_index("patch")
    core = place % 2
    chip = place // 2
    pair = [(i, i ^ 1) for i in range(16)]
    move = lambda a, perm: lax.ppermute(a, "patch", perm)

    sent = fields.reshape(16, 2, 3, PIX, ROWS).transpose(0, 2, 3, 1, 4).reshape(16, 12, 128)
    owned = lax.all_to_all(sent, "var", split_axis=0, concat_axis=0, tiled=True)
    other_weight = move(qkv_weight, pair)
    placing, score, grad_parts, table = call(
        prep_kernel,
        (shape((V * PIX, 256), BF16), shape((V * (PIX + 1), H), F32), shape((H, ROWS, 128), BF16),
         shape((H, 2 * HD, V * (PIX + 1)), BF16)),
        [VM] * 3 + [ANY] * 5, "prep",
        [pltpu.VMEM((V, PIX, D), BF16)] + [pltpu.VMEM((D, D), BF16)] * 2 + [pltpu.VMEM((2, ROWS, D), BF16)]
        + [pltpu.VMEM((D, D), BF16), pltpu.VMEM((H, 2 * HD, V * (PIX + 1)), BF16), pltpu.VMEM((V * PIX, D), F32)]
        + [pltpu.SemaphoreType.DMA((6,))],
        out_specs=(VM, VM, VM, ANY),
    )(var_ids, agg_query, var_embed, embed_weight, agg_value, agg_key, cotangent, out_weight)
    table, other_weight = lax.optimization_barrier((table, other_weight))
    tokens, keep, send = call(
        token_kernel,
        (shape((2 * ROWS, D), F32), shape((ROWS, D), BF16), shape((ROWS, D), BF16)),
        [VM] * 3 + [ANY] * 2 + [VM] + [SM] + [VM] * 2 + [SM], "tokens",
        [pltpu.VMEM((2 * ROWS, D), BF16), pltpu.VMEM((16 * H, 128), BF16), pltpu.VMEM((H, 2 * HD, V * (PIX + 1)), BF16),
         pltpu.VMEM((D, D), BF16), pltpu.SemaphoreType.DMA((2,))],
    )(placing, owned, score, table, agg_out, pos_embed, lead_index, lead_table, norm_gain,
      core.reshape(1))

    here = jnp.concatenate([keep, move(send, pair)], axis=0)
    grad_parts, _ = lax.optimization_barrier((grad_parts, here))
    grad_ctx = lax.all_to_all(grad_parts, "patch", split_axis=0, concat_axis=0, tiled=True)
    shift = lambda a, dx, dy: move(a, [(i, (i + 4 * dx) % 16 ^ (2 * dy)) for i in range(16)])
    left, right, across = shift(here, 1, 0), shift(here, 3, 0), shift(here, 0, 1)
    far0, far1 = shift(left[:64], 1, 0), shift(right[64:], 3, 0)
    left1, right1 = shift(across, 1, 0), shift(across, 3, 0)
    far2, far3 = shift(far0, 0, 1), shift(far1, 0, 1)
    steps = [(1, 0), (3, 0), (0, 1), (2, 0), (1, 1), (3, 1), (2, 1)]
    pieces = [here, left, right, across, far0, far1, left1, right1, far2, far3]
    cx, cy = chip // 2, chip % 2
    chips = []
    for dx, dy in [(0, 0)] + steps:
        chips.append(((cx + 4 - dx) % 4) * 2 + (cy + dy) % 2)
    chips = jnp.stack(chips)
    offsets = (chips[:, None] * 128 + jnp.stack([core, 1 - core])[None, :] * ROWS).reshape(16)

    offsets = offsets.astype(jnp.int32)
    grad_ctx = grad_ctx.reshape(D, 128)
    dest = jnp.stack([((cx + dx) % 4) * 2 + (cy + dy) % 2 for dy in range(2) for dx in range(4)]).reshape(2, 1, 4)
    to = (dest * 128 + jnp.stack([core, 1 - core]).reshape(1, 2, 1) * ROWS).reshape(H).astype(jnp.int32)
    source = jnp.stack([((cx + 4 - dx) % 4) * 2 + (cy + dy) % 2 for dx in range(4) for dy in range(2)]).astype(jnp.int32)
    tall, quarter = pltpu.VMEM((D, 128), BF16), shape((4, ROWS, 128), BF16)
    own, other, *parts = call(
        attention_kernel, (shape((H, 96, 128), BF16),) * 2 + (quarter,) * 4, [ANY] * PIECES + [SM] * 2 + [VM] * 3, "attention",
        [pltpu.VMEM((D, D), BF16)] + [tall] * 4 + [pltpu.VMEM((D, 384), BF16), pltpu.SemaphoreType.DMA((PIECES,))],
    )(*pieces, offsets, to, qkv_weight, other_weight, grad_ctx)
    partial_grad = (own.astype(F32) + move(other, pair).astype(F32)).astype(BF16)
    swap = lambda a, dy, dc: move(a, [(i, i ^ (2 * dy + dc)) for i in range(16)])
    near = [parts[0], swap(parts[1], 0, 1), swap(parts[2], 1, 0), swap(parts[3], 1, 1)]
    sums = lax.all_to_all(partial_grad, "var", split_axis=0, concat_axis=0, tiled=True)
    along = jnp.stack(near, axis=1)
    along = [shift(along[dx], dx, 0) for dx in (1, 2, 3)]
    layer_out = call(
        output_kernel, shape((2 * ROWS, D), BF16), [SM] * 2 + [VM] * 9, "out", [pltpu.VMEM((H // 2, 2 * ROWS, 128), BF16)], mib=8,
    )(source, core.reshape(1), *near, *along, out_weight, tokens)
    grad_qkv = call(sum_kernel, shape((3, ROWS, HD), F32), [VM], "sum", mib=4)(sums)
    return layer_out.reshape(2, ROWS, D), grad_qkv


def solution(mesh):
    in_specs = (
        P(None, "var", None, "patch"), P(), P("var"), P(), P(), P(), P(), P(), P(), P("patch", None), P(), P(),
        P(None, None, "patch"), P(), P("var", "patch", None),
    )
    out_specs = (P("var", "patch", None), P(None, "var", "patch"))
    return jax.shard_map(on_device, mesh=mesh, in_specs=in_specs, out_specs=out_specs, check_vma=False)
```

```python
import functools

import jax
import jax.numpy as jnp
from jax import lax
from jax.experimental import pallas as pl
from jax.experimental.pallas import tpu as pltpu
from jax.sharding import PartitionSpec as P

H = 16
HD = 64
V = 48
PIX = 4
D = 1024
ROWS = 64
F32 = jnp.float32
BF16 = jnp.bfloat16
PIECES = 10
MIB = 1024 * 1024
VMEM_MIB = 58

NN = (((1,), (0,)), ((), ()))
NT = (((1,), (1,)), ((), ()))
TN = (((0,), (0,)), ((), ()))


def mm(a, b, dims=NN):
    return lax.dot_general(a, b, dims, preferred_element_type=F32)


def split2(x):
    high = x.astype(BF16)
    return high, (x - high.astype(F32)).astype(BF16)


def fetch(pairs, sems, first=0):
    copies = [pltpu.make_async_copy(a, b, sems.at[first + i]) for i, (a, b) in enumerate(pairs)]
    for copy in copies:
        copy.start()
    return copies


def prep_kernel(
    ids_ref, query_ref, var_embed_ref, embed_hbm, value_hbm, key_hbm, cot_hbm, out_w_hbm,
    place_ref, score_ref, grad_ref, table_hbm,
    embed_ref, value_ref, key_ref, cot_ref, out_w_ref, table_ref, embed_rows_ref, sems,
):
    copies = fetch(
        [(embed_hbm, embed_ref), (value_hbm, value_ref), (key_hbm, key_ref), (cot_hbm, cot_ref), (out_w_hbm, out_w_ref)], sems
    )
    count = place_ref.shape[1]
    slot = lax.broadcasted_iota(jnp.int32, (V, count), 0)
    col = lax.broadcasted_iota(jnp.int32, (V, count), 1)
    here = ((col // 16) * 3 + (col % 16) // PIX == slot) & (col % 16 < 3 * PIX)
    ids = jnp.broadcast_to(ids_ref[...].reshape(1, V).astype(F32).astype(BF16), (8, V))
    variable = mm(ids, here.astype(F32).astype(BF16))[:1].astype(jnp.int32)
    row = lax.broadcasted_iota(jnp.int32, (V * PIX, count), 0)
    col = lax.broadcasted_iota(jnp.int32, (V * PIX, count), 1)
    match = (variable + V * (col % PIX) == row) & (col % 16 < 3 * PIX)
    place_ref[...] = match.astype(F32).astype(BF16)
    copies[0].wait()
    for n in range(V):
        embed_rows_ref[n * PIX:(n + 1) * PIX, :] = embed_ref[n].astype(F32)
    row = lax.broadcasted_iota(jnp.int32, (V * PIX, V * PIX), 0)
    col = lax.broadcasted_iota(jnp.int32, (V * PIX, V * PIX), 1)
    order = ((row % V) * PIX + row // V == col).astype(F32).astype(BF16)
    table = jnp.concatenate(
        [mm(order, embed_rows_ref[...].astype(BF16)).astype(BF16), var_embed_ref[...]], axis=0
    )
    copies[1].wait()
    values = mm(table, value_ref[...]).T
    high, low = split2(values)
    for h in range(H):
        table_ref[h, :HD, :] = high[h * HD:(h + 1) * HD]
        table_ref[h, HD:, :] = low[h * HD:(h + 1) * HD]
    saved = pltpu.make_async_copy(table_ref, table_hbm, sems.at[5])
    saved.start()
    head = lax.broadcasted_iota(jnp.int32, (H, D), 0)
    feature = lax.broadcasted_iota(jnp.int32, (H, D), 1)
    query = jnp.where(feature // HD == head, query_ref[...].astype(F32).reshape(1, D) * HD ** (-0.5), 0.0)
    copies[2].wait()
    key_query = mm(query.astype(BF16), key_ref[...], NT)
    first = key_query.astype(BF16)
    rest = key_query - first.astype(F32)
    second = rest.astype(BF16)
    third = (rest - second.astype(F32)).astype(BF16)
    score_ref[...] = mm(table, first, NT) + (mm(table, second, NT) + mm(table, third, NT))
    copies[3].wait()
    copies[4].wait()
    grad = mm(cot_ref[...].reshape(2 * ROWS, D), out_w_ref[...], NT).astype(BF16)
    for j in range(H):
        r = (j % 2) * ROWS
        own = grad[r:r + ROWS, j * HD:(j + 1) * HD]
        other = grad[r:r + ROWS, (j ^ 1) * HD:((j ^ 1) + 1) * HD]
        grad_ref[j] = jnp.concatenate([own, other], axis=1)
    saved.wait()


def token_kernel(
    place_ref, fields_ref, score_ref, table_hbm, agg_out_hbm, pos_ref, lead_ref, lead_table_ref, gain_ref,
    core_ref, tokens_ref, keep_ref, send_ref, normed_ref, rows_ref, table_ref, agg_out_ref, sems,
):
    copies = fetch([(table_hbm, table_ref), (agg_out_hbm, agg_out_ref)], sems)
    rows_ref[...] = jnp.zeros_like(rows_ref)
    for j in range(H):
        rows_ref[16 * j:16 * j + 3 * PIX, :] = fields_ref[j]
    pixels = mm(place_ref[...], rows_ref[...])
    parts = [pixels[k * V:(k + 1) * V] for k in range(PIX)]
    mixed = []
    for h in range(H):
        column = lambda k: score_ref[k * V:(k + 1) * V, h:h + 1]
        scores = column(PIX) + parts[0] * column(0)
        for k in range(1, PIX):
            scores = scores + parts[k] * column(k)
        probs = jnp.exp(scores - jnp.max(scores, axis=0, keepdims=True))
        probs = probs / jnp.sum(probs, axis=0, keepdims=True)
        mixing = jnp.concatenate([probs * part for part in parts] + [probs], axis=0)
        mixed.append(split2(mixing))
    copies[0].wait()
    pooled = []
    for h in range(H):
        high, low = mixed[h]
        both = mm(table_ref[h], high)
        pooled.append((both[:HD] + (both[HD:] + mm(table_ref[h, :HD], low))).astype(BF16))
    pooled = jnp.concatenate(pooled, axis=0)
    copies[1].wait()
    tokens = mm(pooled, agg_out_ref[...], TN)
    row = lax.broadcasted_iota(jnp.int32, (2 * ROWS, 16), 0)
    col = lax.broadcasted_iota(jnp.int32, (2 * ROWS, 16), 1)
    lead = jnp.where(row < ROWS, lead_ref[0], lead_ref[1])
    lead_rows = mm((lead == col).astype(F32).astype(BF16), lead_table_ref[...])
    pos = pos_ref[...].astype(F32)
    tokens = tokens + jnp.concatenate([pos, pos], axis=0) + lead_rows
    tokens_ref[...] = tokens
    center = tokens - jnp.mean(tokens, axis=-1, keepdims=True)
    spread = jnp.mean(center * center, axis=-1, keepdims=True)
    normed_ref[...] = (center * lax.rsqrt(spread + 1e-05) * gain_ref[...].astype(F32).reshape(1, D)).astype(BF16)
    core = core_ref[0] % 2
    own = pl.multiple_of(core * ROWS, ROWS)
    other = pl.multiple_of((1 - core) * ROWS, ROWS)
    keep_ref[...] = normed_ref[pl.ds(own, ROWS), :]
    send_ref[...] = normed_ref[pl.ds(other, ROWS), :]


def softmax_of(keys, queries):
    scores = mm(keys, queries, NT)
    e = jnp.exp(scores - jnp.max(scores, axis=0, keepdims=True))
    return e * (1.0 / jnp.sum(e, axis=0, keepdims=True))


def head_of(x, h):
    lane = lax.broadcasted_iota(jnp.int32, x.shape, 1)
    return jnp.where(lane // HD == h, x, jnp.zeros_like(x))


STEPS = [(0, 0), (1, 0), (3, 0), (0, 1), (2, 0), (1, 1), (3, 1), (2, 1)]


def chip_at(place, dx, dy):
    chip = place // 2
    return (chip // 2 + dx) % 4 * 2 + (chip + dy) % 2


def gather_rows(pieces, x_ref):
    pairs, at = [], 0
    for piece in pieces:
        pairs.append((piece, x_ref.at[pl.ds(at, piece.shape[0])]))
        at += piece.shape[0]
    return pairs


def project_kernel(*refs):
    pieces = refs[:PIECES - 2]
    own_w_ref, other_w_ref, out_ref, x_ref, sems = refs[PIECES - 2:]
    copies = fetch(gather_rows(pieces, x_ref), sems)
    weight = jnp.concatenate([w for i in range(3) for w in (own_w_ref[i], other_w_ref[i])], axis=0)
    for copy in copies:
        copy.wait()
    out_ref[...] = mm(x_ref[...], weight, NT).astype(BF16)


def attention_kernel(*refs):
    pieces = refs[:PIECES]
    place_ref, projected_hbm, own_w_ref, other_w_ref, grad_ctx_ref, own_ref, other_ref = refs[PIECES:PIECES + 7]
    part_refs = refs[PIECES + 7:PIECES + 11]
    x_ref, projected_ref, context_ref, q_ref, k_ref, v_ref, rows_ref, sems = refs[PIECES + 11:]
    place = place_ref[0]
    core = place % 2
    rows_at = lambda dx, dy, s: pl.ds(pl.multiple_of(chip_at(place, dx, dy) * 128 + jnp.abs(core - s) * ROWS, ROWS), ROWS)
    offsets = [rows_at(4 - dx, dy, s) for dx, dy in STEPS for s in range(2)]
    done = D - 2 * ROWS
    pairs = gather_rows(pieces, x_ref)
    copies = fetch([(projected_hbm, projected_ref.at[pl.ds(0, done)])] + pairs[-2:] + pairs[:-2], sems)
    weight = jnp.concatenate([w for i in range(3) for w in (own_w_ref[i], other_w_ref[i])], axis=0)
    for copy in copies[:3]:
        copy.wait()
    projected_ref[done:, :] = mm(x_ref[done:, :], weight, NT).astype(BF16)
    projected = projected_ref[...]
    for i in range(H):
        rows = offsets[i]
        here = projected[i * ROWS:(i + 1) * ROWS]
        q_ref[rows, :] = here[:, :128] * jnp.asarray(HD ** (-0.5), BF16)
        k_ref[rows, :] = here[:, 128:256]
        v_ref[rows, :] = here[:, 256:]
    keys, values = k_ref[...], v_ref[...]
    keys_t, values_t = keys.T, values.T
    context, dq, low, ds, gs, qs = [], [], [], [], [], []
    for h in range(2):
        queries = head_of(q_ref[...], h)
        grads = head_of(grad_ctx_ref[...], h)
        probs = softmax_of(keys, queries)
        probs_low = probs.astype(BF16)
        context.append(mm(values_t[h * HD:(h + 1) * HD], probs_low))
        dp = mm(values, grads, NT)
        dots = jnp.sum(probs * dp, axis=0, keepdims=True)
        d = (probs * (dp - dots)).astype(BF16)
        dq.append(mm(keys_t[h * HD:(h + 1) * HD], d))
        low.append(probs_low)
        ds.append(d)
        gs.append(grads)
        qs.append(queries)
    context_ref[...] = jnp.concatenate(context, axis=0).T.astype(BF16)
    for i in range(H):
        part_refs[i // 4][i % 4] = context_ref[rows_at(i % 4, i // 8, i // 4 % 2), :]
    dq = (jnp.concatenate(dq, axis=0).T * HD ** (-0.5)).astype(BF16)
    dv = mm(jnp.concatenate(low, axis=1), jnp.concatenate(gs, axis=0)).astype(BF16)
    dk = mm(jnp.concatenate(ds, axis=1), jnp.concatenate(qs, axis=0)).astype(BF16)
    rows_ref[:, :128] = jnp.concatenate([dq[:, :HD], dk[:, :HD]], axis=1)
    rows_ref[:, 128:256] = jnp.concatenate([dq[:, HD:], dk[:, HD:]], axis=1)
    rows_ref[:, 256:] = dv
    order = jnp.concatenate([rows_ref[rows, :] for rows in offsets], axis=0)
    for copy in copies[3:]:
        copy.wait()
    grad = mm(x_ref[...], order, TN).astype(BF16)
    for j in range(H):
        top = grad[j * ROWS:j * ROWS + ROWS // 2, 256:]
        bottom = grad[j * ROWS + ROWS // 2:(j + 1) * ROWS, 256:]
        own_ref[j, :ROWS] = grad[j * ROWS:(j + 1) * ROWS, :128]
        own_ref[j, ROWS:] = jnp.concatenate([top[:, :HD], bottom[:, :HD]], axis=1)
        other_ref[j, :ROWS] = grad[j * ROWS:(j + 1) * ROWS, 128:256]
        other_ref[j, ROWS:] = jnp.concatenate([top[:, HD:], bottom[:, HD:]], axis=1)


def output_kernel(place_ref, *refs):
    near = refs[:4]
    along = refs[4:7]
    out_w_ref, tokens_ref, out_ref, context_ref = refs[7:]
    place = place_ref[0]
    core = place % 2
    for dx in range(4):
        for i in range(4):
            part = along[dx - 1][i] if dx else near[i][0]
            sample = core if i % 2 == 0 else 1 - core
            part = jnp.where(sample == 1, jnp.concatenate([part[:, HD:], part[:, :HD]], axis=1), part)
            context_ref[chip_at(place, 4 - dx, i // 2), pl.ds(pl.multiple_of(sample * ROWS, ROWS), ROWS), :] = part
    context = jnp.concatenate([context_ref[m] for m in range(H // 2)], axis=1)
    out_ref[...] = (tokens_ref[...] + mm(context, out_w_ref[...])).astype(BF16)


def add_kernel(a_ref, b_ref, out_ref):
    out_ref[...] = (a_ref[...].astype(F32) + b_ref[...].astype(F32)).astype(BF16)


def sum_kernel(parts_ref, out_ref):
    total = parts_ref[0].astype(F32)
    for j in range(1, H):
        total = total + parts_ref[j].astype(F32)
    out_ref[0] = total[:ROWS, :HD]
    out_ref[1] = total[:ROWS, HD:]
    out_ref[2, :ROWS // 2] = total[ROWS:, :HD]
    out_ref[2, ROWS // 2:] = total[ROWS:, HD:]


VM = pl.BlockSpec(memory_space=pltpu.VMEM)
SM = pl.BlockSpec(memory_space=pltpu.SMEM)
ANY = pl.BlockSpec(memory_space=pl.ANY)


def call(kernel, out, in_specs, name, scratch=(), out_specs=None, mib=VMEM_MIB):
    return pl.pallas_call(
        kernel,
        out_shape=out,
        in_specs=in_specs,
        out_specs=out_specs or jax.tree.map(lambda _: VM, out),
        scratch_shapes=list(scratch),
        compiler_params=pltpu.CompilerParams(vmem_limit_bytes=mib * MIB),
        name=name,
    )


def shape(dims, dtype):
    return jax.ShapeDtypeStruct(dims, dtype)


def on_device(
    fields, var_ids, lead_index, embed_weight, var_embed, agg_query, agg_key, agg_value, agg_out,
    pos_embed, lead_table, norm_gain, qkv_weight, out_weight, cotangent,
):
    place = lax.axis_index("patch")
    pair = [(i, i ^ 1) for i in range(16)]
    move = lambda a, perm: lax.ppermute(a, "patch", perm)

    sent = fields.reshape(16, 2, 3, PIX, ROWS).transpose(0, 2, 3, 1, 4).reshape(16, 12, 128)
    owned = lax.all_to_all(sent, "var", split_axis=0, concat_axis=0, tiled=True)
    own_weight = qkv_weight.transpose(0, 2, 1)
    other_weight = move(own_weight, pair)
    placing, score, grad_parts, table = call(
        prep_kernel,
        (shape((V * PIX, 256), BF16), shape((V * (PIX + 1), H), F32), shape((H, ROWS, 128), BF16),
         shape((H, 2 * HD, V * (PIX + 1)), BF16)),
        [VM] * 3 + [ANY] * 5, "prep",
        [pltpu.VMEM((V, PIX, D), BF16)] + [pltpu.VMEM((D, D), BF16)] * 2 + [pltpu.VMEM((2, ROWS, D), BF16)]
        + [pltpu.VMEM((D, D), BF16), pltpu.VMEM((H, 2 * HD, V * (PIX + 1)), BF16), pltpu.VMEM((V * PIX, D), F32)]
        + [pltpu.SemaphoreType.DMA((6,))],
        out_specs=(VM, VM, VM, ANY),
    )(var_ids, agg_query, var_embed, embed_weight, agg_value, agg_key, cotangent, out_weight)
    table, other_weight = lax.optimization_barrier((table, other_weight))
    tokens, keep, send = call(
        token_kernel,
        (shape((2 * ROWS, D), F32), shape((ROWS, D), BF16), shape((ROWS, D), BF16)),
        [VM] * 3 + [ANY] * 2 + [VM] + [SM] + [VM] * 2 + [SM], "tokens",
        [pltpu.VMEM((2 * ROWS, D), BF16), pltpu.VMEM((16 * H, 128), BF16), pltpu.VMEM((H, 2 * HD, V * (PIX + 1)), BF16),
         pltpu.VMEM((D, D), BF16), pltpu.SemaphoreType.DMA((2,))],
    )(placing, owned, score, table, agg_out, pos_embed, lead_index, lead_table, norm_gain,
      place.reshape(1))

    here = jnp.concatenate([keep, move(send, pair)], axis=0)
    grad_parts, _ = lax.optimization_barrier((grad_parts, here))
    grad_ctx = lax.all_to_all(grad_parts, "patch", split_axis=0, concat_axis=0, tiled=True)
    shift = lambda a, dx, dy: move(a, [(i, (i + 4 * dx) % 16 ^ (2 * dy)) for i in range(16)])
    left, right, across = shift(here, 1, 0), shift(here, 3, 0), shift(here, 0, 1)
    far0, far1 = shift(left[:64], 1, 0), shift(right[64:], 3, 0)
    left1, right1 = shift(across, 1, 0), shift(across, 3, 0)
    far0, far1, grad_ctx = lax.optimization_barrier((far0, far1, grad_ctx))
    far2, far3 = shift(far0, 0, 1), shift(far1, 0, 1)
    pieces = [here, left, right, across, far0, far1, left1, right1, far2, far3]
    grad_ctx = grad_ctx.reshape(D, 128)
    tall, quarter = pltpu.VMEM((D, 128), BF16), shape((4, ROWS, 128), BF16)
    projected = call(
        project_kernel, shape((D - 2 * ROWS, 384), BF16), [ANY] * (PIECES - 2) + [VM] * 2, "project",
        [pltpu.VMEM((D - 2 * ROWS, D), BF16), pltpu.SemaphoreType.DMA((PIECES - 2,))],
    )(*pieces[:-2], own_weight, other_weight)
    own, other, *parts = call(
        attention_kernel, (shape((H, 96, 128), BF16),) * 2 + (quarter,) * 4, [ANY] * PIECES + [SM, ANY] + [VM] * 3, "attention",
        [pltpu.VMEM((D, D), BF16), pltpu.VMEM((D, 384), BF16)] + [tall] * 4 + [pltpu.VMEM((D, 384), BF16), pltpu.SemaphoreType.DMA((PIECES + 1,))],
    )(*pieces, place.reshape(1), projected, own_weight, other_weight, grad_ctx)
    partial_grad = call(add_kernel, shape((H, 96, 128), BF16), [VM] * 2, "add", mib=4)(own, move(other, pair))
    swap = lambda a, dy, dc: move(a, [(i, i ^ (2 * dy + dc)) for i in range(16)])
    near = [parts[0], swap(parts[1], 0, 1), swap(parts[2], 1, 0), swap(parts[3], 1, 1)]
    sums = lax.all_to_all(partial_grad, "var", split_axis=0, concat_axis=0, tiled=True)
    along = jnp.stack(near, axis=1)
    along = [shift(along[dx], dx, 0) for dx in (1, 2, 3)]
    layer_out = call(
        output_kernel, shape((2 * ROWS, D), BF16), [SM] + [VM] * 9, "out", [pltpu.VMEM((H // 2, 2 * ROWS, 128), BF16)], mib=8,
    )(place.reshape(1), *near, *along, out_weight, tokens)
    grad_qkv = call(sum_kernel, shape((3, ROWS, HD), F32), [VM], "sum", mib=4)(sums)
    return layer_out.reshape(2, ROWS, D), grad_qkv


def solution(mesh):
    in_specs = (
        P(None, "var", None, "patch"), P(), P("var"), P(), P(), P(), P(), P(), P(), P("patch", None), P(), P(),
        P(None, None, "patch"), P(), P("var", "patch", None),
    )
    out_specs = (P("var", "patch", None), P(None, "var", "patch"))
    return jax.shard_map(on_device, mesh=mesh, in_specs=in_specs, out_specs=out_specs, check_vma=False)
```

```python
import functools

import jax
import jax.numpy as jnp
from jax import lax
from jax.experimental import pallas as pl
from jax.experimental.pallas import tpu as pltpu
from jax.sharding import PartitionSpec as P

H = 16
HD = 64
V = 48
PIX = 4
D = 1024
ROWS = 64
F32 = jnp.float32
BF16 = jnp.bfloat16
PIECES = 10
MIB = 1024 * 1024
VMEM_MIB = 58

NN = (((1,), (0,)), ((), ()))
NT = (((1,), (1,)), ((), ()))
TN = (((0,), (0,)), ((), ()))


def mm(a, b, dims=NN):
    return lax.dot_general(a, b, dims, preferred_element_type=F32)


def split2(x):
    high = x.astype(BF16)
    return high, (x - high.astype(F32)).astype(BF16)


def fetch(pairs, sems, first=0):
    copies = [pltpu.make_async_copy(a, b, sems.at[first + i]) for i, (a, b) in enumerate(pairs)]
    for copy in copies:
        copy.start()
    return copies


def prep_kernel(
    ids_ref, query_ref, var_embed_ref, embed_hbm, value_hbm, key_hbm, cot_hbm, out_w_hbm,
    place_ref, score_ref, grad_ref, table_hbm,
    embed_ref, value_ref, key_ref, cot_ref, out_w_ref, table_ref, embed_rows_ref, sems,
):
    copies = fetch(
        [(embed_hbm, embed_ref), (value_hbm, value_ref), (key_hbm, key_ref), (cot_hbm, cot_ref), (out_w_hbm, out_w_ref)], sems
    )
    count = place_ref.shape[1]
    slot = lax.broadcasted_iota(jnp.int32, (V, count), 0)
    col = lax.broadcasted_iota(jnp.int32, (V, count), 1)
    here = ((col // 16) * 3 + (col % 16) // PIX == slot) & (col % 16 < 3 * PIX)
    ids = jnp.broadcast_to(ids_ref[...].reshape(1, V).astype(F32).astype(BF16), (8, V))
    variable = mm(ids, here.astype(F32).astype(BF16))[:1].astype(jnp.int32)
    row = lax.broadcasted_iota(jnp.int32, (V * PIX, count), 0)
    col = lax.broadcasted_iota(jnp.int32, (V * PIX, count), 1)
    match = (variable + V * (col % PIX) == row) & (col % 16 < 3 * PIX)
    place_ref[...] = match.astype(F32).astype(BF16)
    copies[0].wait()
    for n in range(V):
        embed_rows_ref[n * PIX:(n + 1) * PIX, :] = embed_ref[n].astype(F32)
    row = lax.broadcasted_iota(jnp.int32, (V * PIX, V * PIX), 0)
    col = lax.broadcasted_iota(jnp.int32, (V * PIX, V * PIX), 1)
    order = ((row % V) * PIX + row // V == col).astype(F32).astype(BF16)
    table = jnp.concatenate(
        [mm(order, embed_rows_ref[...].astype(BF16)).astype(BF16), var_embed_ref[...]], axis=0
    )
    copies[1].wait()
    values = mm(table, value_ref[...]).T
    high, low = split2(values)
    for h in range(H):
        table_ref[h, :HD, :] = high[h * HD:(h + 1) * HD]
        table_ref[h, HD:, :] = low[h * HD:(h + 1) * HD]
    saved = pltpu.make_async_copy(table_ref, table_hbm, sems.at[5])
    saved.start()
    head = lax.broadcasted_iota(jnp.int32, (H, D), 0)
    feature = lax.broadcasted_iota(jnp.int32, (H, D), 1)
    query = jnp.where(feature // HD == head, query_ref[...].astype(F32).reshape(1, D) * HD ** (-0.5), 0.0)
    copies[2].wait()
    key_query = mm(query.astype(BF16), key_ref[...], NT)
    first = key_query.astype(BF16)
    rest = key_query - first.astype(F32)
    second = rest.astype(BF16)
    third = (rest - second.astype(F32)).astype(BF16)
    score_ref[...] = mm(table, first, NT) + (mm(table, second, NT) + mm(table, third, NT))
    copies[3].wait()
    copies[4].wait()
    grad = mm(cot_ref[...].reshape(2 * ROWS, D), out_w_ref[...], NT).astype(BF16)
    for j in range(H):
        r = (j % 2) * ROWS
        own = grad[r:r + ROWS, j * HD:(j + 1) * HD]
        other = grad[r:r + ROWS, (j ^ 1) * HD:((j ^ 1) + 1) * HD]
        grad_ref[j] = jnp.concatenate([own, other], axis=1)
    saved.wait()


def token_kernel(
    place_ref, fields_ref, score_ref, table_hbm, agg_out_hbm, pos_ref, lead_ref, lead_table_ref, gain_ref,
    core_ref, tokens_ref, keep_ref, send_ref, normed_ref, rows_ref, table_ref, agg_out_ref, sems,
):
    copies = fetch([(table_hbm, table_ref), (agg_out_hbm, agg_out_ref)], sems)
    rows_ref[...] = jnp.zeros_like(rows_ref)
    for j in range(H):
        rows_ref[16 * j:16 * j + 3 * PIX, :] = fields_ref[j]
    pixels = mm(place_ref[...], rows_ref[...])
    parts = [pixels[k * V:(k + 1) * V] for k in range(PIX)]
    mixed = []
    for h in range(H):
        column = lambda k: score_ref[k * V:(k + 1) * V, h:h + 1]
        scores = column(PIX) + parts[0] * column(0)
        for k in range(1, PIX):
            scores = scores + parts[k] * column(k)
        probs = jnp.exp(scores - jnp.max(scores, axis=0, keepdims=True))
        probs = probs / jnp.sum(probs, axis=0, keepdims=True)
        mixing = jnp.concatenate([probs * part for part in parts] + [probs], axis=0)
        mixed.append(split2(mixing))
    copies[0].wait()
    pooled = []
    for h in range(H):
        high, low = mixed[h]
        both = mm(table_ref[h], high)
        pooled.append((both[:HD] + (both[HD:] + mm(table_ref[h, :HD], low))).astype(BF16))
    pooled = jnp.concatenate(pooled, axis=0)
    copies[1].wait()
    tokens = mm(pooled, agg_out_ref[...], TN)
    row = lax.broadcasted_iota(jnp.int32, (2 * ROWS, 16), 0)
    col = lax.broadcasted_iota(jnp.int32, (2 * ROWS, 16), 1)
    lead = jnp.where(row < ROWS, lead_ref[0], lead_ref[1])
    lead_rows = mm((lead == col).astype(F32).astype(BF16), lead_table_ref[...])
    pos = pos_ref[...].astype(F32)
    tokens = tokens + jnp.concatenate([pos, pos], axis=0) + lead_rows
    tokens_ref[...] = tokens
    center = tokens - jnp.mean(tokens, axis=-1, keepdims=True)
    spread = jnp.mean(center * center, axis=-1, keepdims=True)
    normed_ref[...] = (center * lax.rsqrt(spread + 1e-05) * gain_ref[...].astype(F32).reshape(1, D)).astype(BF16)
    core = core_ref[0] % 2
    own = pl.multiple_of(core * ROWS, ROWS)
    other = pl.multiple_of((1 - core) * ROWS, ROWS)
    keep_ref[...] = normed_ref[pl.ds(own, ROWS), :]
    send_ref[...] = normed_ref[pl.ds(other, ROWS), :]


def softmax_of(keys, queries):
    scores = mm(keys, queries, NT)
    e = jnp.exp(scores - jnp.max(scores, axis=0, keepdims=True))
    return e * (1.0 / jnp.sum(e, axis=0, keepdims=True))


def head_of(x, h):
    lane = lax.broadcasted_iota(jnp.int32, x.shape, 1)
    return jnp.where(lane // HD == h, x, jnp.zeros_like(x))


STEPS = [(0, 0), (1, 0), (3, 0), (0, 1), (2, 0), (1, 1), (3, 1), (2, 1)]


def chip_at(place, dx, dy):
    chip = place // 2
    return (chip // 2 + dx) % 4 * 2 + (chip + dy) % 2


def gather_rows(pieces, x_ref):
    pairs, at = [], 0
    for piece in pieces:
        pairs.append((piece, x_ref.at[pl.ds(at, piece.shape[0])]))
        at += piece.shape[0]
    return pairs


def attention_kernel(*refs):
    pieces = refs[:PIECES]
    place_ref, own_w_ref, other_w_ref, grad_ctx_ref, own_ref, other_ref = refs[PIECES:PIECES + 6]
    part_refs = refs[PIECES + 6:PIECES + 10]
    x_ref, context_ref, q_ref, k_ref, v_ref, rows_ref, sems = refs[PIECES + 10:]
    place = place_ref[0]
    core = place % 2
    rows_at = lambda dx, dy, s: pl.ds(pl.multiple_of(chip_at(place, dx, dy) * 128 + jnp.abs(core - s) * ROWS, ROWS), ROWS)
    offsets = [rows_at(4 - dx, dy, s) for dx, dy in STEPS for s in range(2)]
    copies = fetch(gather_rows(pieces, x_ref), sems)
    weight = jnp.concatenate([w for i in range(3) for w in (own_w_ref[i], other_w_ref[i])], axis=0)
    for copy in copies:
        copy.wait()
    projected = mm(x_ref[...], weight, NT).astype(BF16)
    for i in range(H):
        rows = offsets[i]
        here = projected[i * ROWS:(i + 1) * ROWS]
        q_ref[rows, :] = here[:, :128] * jnp.asarray(HD ** (-0.5), BF16)
        k_ref[rows, :] = here[:, 128:256]
        v_ref[rows, :] = here[:, 256:]
    keys, values = k_ref[...], v_ref[...]
    keys_t, values_t = keys.T, values.T
    context, dq, low, ds, gs, qs = [], [], [], [], [], []
    for h in range(2):
        queries = head_of(q_ref[...], h)
        grads = head_of(grad_ctx_ref[...], h)
        probs = softmax_of(keys, queries)
        probs_low = probs.astype(BF16)
        context.append(mm(values_t[h * HD:(h + 1) * HD], probs_low))
        dp = mm(values, grads, NT)
        dots = jnp.sum(probs * dp, axis=0, keepdims=True)
        d = (probs * (dp - dots)).astype(BF16)
        dq.append(mm(keys_t[h * HD:(h + 1) * HD], d))
        low.append(probs_low)
        ds.append(d)
        gs.append(grads)
        qs.append(queries)
    context_ref[...] = jnp.concatenate(context, axis=0).T.astype(BF16)
    for i in range(H):
        part_refs[i // 4][i % 4] = context_ref[rows_at(i % 4, i // 8, i // 4 % 2), :]
    dq = (jnp.concatenate(dq, axis=0).T * HD ** (-0.5)).astype(BF16)
    dv = mm(jnp.concatenate(low, axis=1), jnp.concatenate(gs, axis=0)).astype(BF16)
    dk = mm(jnp.concatenate(ds, axis=1), jnp.concatenate(qs, axis=0)).astype(BF16)
    rows_ref[:, :128] = jnp.concatenate([dq[:, :HD], dk[:, :HD]], axis=1)
    rows_ref[:, 128:256] = jnp.concatenate([dq[:, HD:], dk[:, HD:]], axis=1)
    rows_ref[:, 256:] = dv
    order = jnp.concatenate([rows_ref[rows, :] for rows in offsets], axis=0)
    grad = mm(x_ref[...], order, TN).astype(BF16)
    for j in range(H):
        top = grad[j * ROWS:j * ROWS + ROWS // 2, 256:]
        bottom = grad[j * ROWS + ROWS // 2:(j + 1) * ROWS, 256:]
        own_ref[j, :ROWS] = grad[j * ROWS:(j + 1) * ROWS, :128]
        own_ref[j, ROWS:] = jnp.concatenate([top[:, :HD], bottom[:, :HD]], axis=1)
        other_ref[j, :ROWS] = grad[j * ROWS:(j + 1) * ROWS, 128:256]
        other_ref[j, ROWS:] = jnp.concatenate([top[:, HD:], bottom[:, HD:]], axis=1)


def output_kernel(place_ref, *refs):
    near = refs[:4]
    along = refs[4:7]
    out_w_ref, tokens_ref, out_ref, context_ref = refs[7:]
    place = place_ref[0]
    core = place % 2
    for dx in range(4):
        for i in range(4):
            part = along[dx - 1][i] if dx else near[i][0]
            sample = core if i % 2 == 0 else 1 - core
            part = jnp.where(sample == 1, jnp.concatenate([part[:, HD:], part[:, :HD]], axis=1), part)
            context_ref[chip_at(place, 4 - dx, i // 2), pl.ds(pl.multiple_of(sample * ROWS, ROWS), ROWS), :] = part
    context = jnp.concatenate([context_ref[m] for m in range(H // 2)], axis=1)
    out_ref[...] = (tokens_ref[...] + mm(context, out_w_ref[...])).astype(BF16)


def add_kernel(a_ref, b_ref, out_ref):
    out_ref[...] = (a_ref[...].astype(F32) + b_ref[...].astype(F32)).astype(BF16)


def sum_kernel(parts_ref, out_ref):
    total = parts_ref[0].astype(F32)
    for j in range(1, H):
        total = total + parts_ref[j].astype(F32)
    out_ref[0] = total[:ROWS, :HD]
    out_ref[1] = total[:ROWS, HD:]
    out_ref[2, :ROWS // 2] = total[ROWS:, :HD]
    out_ref[2, ROWS // 2:] = total[ROWS:, HD:]


VM = pl.BlockSpec(memory_space=pltpu.VMEM)
SM = pl.BlockSpec(memory_space=pltpu.SMEM)
ANY = pl.BlockSpec(memory_space=pl.ANY)


def call(kernel, out, in_specs, name, scratch=(), out_specs=None, mib=VMEM_MIB):
    return pl.pallas_call(
        kernel,
        out_shape=out,
        in_specs=in_specs,
        out_specs=out_specs or jax.tree.map(lambda _: VM, out),
        scratch_shapes=list(scratch),
        compiler_params=pltpu.CompilerParams(vmem_limit_bytes=mib * MIB),
        name=name,
    )


def shape(dims, dtype):
    return jax.ShapeDtypeStruct(dims, dtype)


def on_device(
    fields, var_ids, lead_index, embed_weight, var_embed, agg_query, agg_key, agg_value, agg_out,
    pos_embed, lead_table, norm_gain, qkv_weight, out_weight, cotangent,
):
    place = lax.axis_index("patch")
    pair = [(i, i ^ 1) for i in range(16)]
    move = lambda a, perm: lax.ppermute(a, "patch", perm)

    sent = fields.reshape(16, 2, 3, PIX, ROWS).transpose(0, 2, 3, 1, 4).reshape(16, 12, 128)
    owned = lax.all_to_all(sent, "var", split_axis=0, concat_axis=0, tiled=True)
    own_weight = qkv_weight.transpose(0, 2, 1)
    other_weight = move(own_weight, pair)
    placing, score, grad_parts, table = call(
        prep_kernel,
        (shape((V * PIX, 256), BF16), shape((V * (PIX + 1), H), F32), shape((H, ROWS, 128), BF16),
         shape((H, 2 * HD, V * (PIX + 1)), BF16)),
        [VM] * 3 + [ANY] * 5, "prep",
        [pltpu.VMEM((V, PIX, D), BF16)] + [pltpu.VMEM((D, D), BF16)] * 2 + [pltpu.VMEM((2, ROWS, D), BF16)]
        + [pltpu.VMEM((D, D), BF16), pltpu.VMEM((H, 2 * HD, V * (PIX + 1)), BF16), pltpu.VMEM((V * PIX, D), F32)]
        + [pltpu.SemaphoreType.DMA((6,))],
        out_specs=(VM, VM, VM, ANY),
    )(var_ids, agg_query, var_embed, embed_weight, agg_value, agg_key, cotangent, out_weight)
    table, other_weight = lax.optimization_barrier((table, other_weight))
    tokens, keep, send = call(
        token_kernel,
        (shape((2 * ROWS, D), F32), shape((ROWS, D), BF16), shape((ROWS, D), BF16)),
        [VM] * 3 + [ANY] * 2 + [VM] + [SM] + [VM] * 2 + [SM], "tokens",
        [pltpu.VMEM((2 * ROWS, D), BF16), pltpu.VMEM((16 * H, 128), BF16), pltpu.VMEM((H, 2 * HD, V * (PIX + 1)), BF16),
         pltpu.VMEM((D, D), BF16), pltpu.SemaphoreType.DMA((2,))],
    )(placing, owned, score, table, agg_out, pos_embed, lead_index, lead_table, norm_gain,
      place.reshape(1))

    here = jnp.concatenate([keep, move(send, pair)], axis=0)
    grad_parts, _ = lax.optimization_barrier((grad_parts, here))
    grad_ctx = lax.all_to_all(grad_parts, "patch", split_axis=0, concat_axis=0, tiled=True)
    shift = lambda a, dx, dy: move(a, [(i, (i + 4 * dx) % 16 ^ (2 * dy)) for i in range(16)])
    left, right, across = shift(here, 1, 0), shift(here, 3, 0), shift(here, 0, 1)
    far0, far1 = shift(left[:64], 1, 0), shift(right[64:], 3, 0)
    left1, right1 = shift(across, 1, 0), shift(across, 3, 0)
    far0, far1, grad_ctx = lax.optimization_barrier((far0, far1, grad_ctx))
    far2, far3 = shift(far0, 0, 1), shift(far1, 0, 1)
    pieces = [here, left, right, across, far0, far1, left1, right1, far2, far3]
    grad_ctx = grad_ctx.reshape(D, 128)
    tall, quarter = pltpu.VMEM((D, 128), BF16), shape((4, ROWS, 128), BF16)
    own, other, *parts = call(
        attention_kernel, (shape((H, 96, 128), BF16),) * 2 + (quarter,) * 4, [ANY] * PIECES + [SM] + [VM] * 3, "attention",
        [pltpu.VMEM((D, D), BF16)] + [tall] * 4 + [pltpu.VMEM((D, 384), BF16), pltpu.SemaphoreType.DMA((PIECES,))],
    )(*pieces, place.reshape(1), own_weight, other_weight, grad_ctx)
    partial_grad = call(add_kernel, shape((H, 96, 128), BF16), [VM] * 2, "add", mib=4)(own, move(other, pair))
    swap = lambda a, dy, dc: move(a, [(i, i ^ (2 * dy + dc)) for i in range(16)])
    near = [parts[0], swap(parts[1], 0, 1), swap(parts[2], 1, 0), swap(parts[3], 1, 1)]
    sums = lax.all_to_all(partial_grad, "var", split_axis=0, concat_axis=0, tiled=True)
    along = jnp.stack(near, axis=1)
    along = [shift(along[dx], dx, 0) for dx in (1, 2, 3)]
    layer_out = call(
        output_kernel, shape((2 * ROWS, D), BF16), [SM] + [VM] * 9, "out", [pltpu.VMEM((H // 2, 2 * ROWS, 128), BF16)], mib=8,
    )(place.reshape(1), *near, *along, out_weight, tokens)
    grad_qkv = call(sum_kernel, shape((3, ROWS, HD), F32), [VM], "sum", mib=4)(sums)
    return layer_out.reshape(2, ROWS, D), grad_qkv


def solution(mesh):
    in_specs = (
        P(None, "var", None, "patch"), P(), P("var"), P(), P(), P(), P(), P(), P(), P("patch", None), P(), P(),
        P(None, None, "patch"), P(), P("var", "patch", None),
    )
    out_specs = (P("var", "patch", None), P(None, "var", "patch"))
    return jax.shard_map(on_device, mesh=mesh, in_specs=in_specs, out_specs=out_specs, check_vma=False)
```
